1024 devices in a mesh: gx: 64 (over y_hi, z), gy: 16 (over x, y_lo, core).
Axes of the slice: x: 4, y: 4 (y_hi: 2, y_lo: 2; y = y_hi * 2 + y_lo), z: 32, core: 2. Of those that a mesh axis runs over, the one named last changes fastest.
Arguments:
- state: bfloat16 [128, 16, 128, 256], P('gx', 'gy'), may hold values from -6 to 6
- species: int32 [128, 16, 128], P('gx', 'gy'), may hold values from 0 to 3
- species_bias: float32 [4, 256], replicated, may hold values from -4 to 4
- edge_index: int32 [128, 16, 2, 512], P('gx', 'gy'), may hold values from 0 to 1151, as said below
- edge_count: int32 [128, 16], P('gx', 'gy'), may hold values from 128 to 512, as said below
- edge_dist: float32 [128, 16, 512], P('gx', 'gy'), may hold values from 0.2 to 0.9
- trip_index: int32 [128, 16, 2, 1024], P('gx', 'gy'), may hold values from 0 to 511, as said below
- trip_count: int32 [128, 16], P('gx', 'gy'), may hold values from 256 to 1024, as said below
- trip_cos: float32 [128, 16, 1024], P('gx', 'gy'), may hold values from -1 to 1
- radial_weight: float32 [256], replicated, may hold values from -4 to 4
- norm_gain: float32 [256], replicated, may hold values from 0.1 to 1.9
- w_centre: bfloat16 [256, 256], replicated, may hold values from -0.375 to 0.375
- w_neigh: bfloat16 [256, 256], replicated, may hold values from -0.375 to 0.375
- w_mix: bfloat16 [256, 256], replicated, may hold values from -0.375 to 0.375
- w_out: bfloat16 [256, 256], replicated, may hold values from -0.375 to 0.375
Outputs:
- updated: bfloat16 [128, 16, 128, 256], P('gx', 'gy')
The draws below stay inside these ranges and needn't reach their ends.
Inputs may be any that keep to these rules, and one draw needn't show every extreme that they name: `edge_index`: row 0 holds centre slots below 128; row 1 holds neighbour codes cell * 128 + slot with cell from 0 to 8 and slot below 128; slots at or past the tile's edge_count are padding of arbitrary such values. `edge_count`: some tile has all 512 slots live. `trip_index`: in live slots both rows name live edges of the same tile and differ; padding slots follow the same rule. `trip_count`: some tile has all 1024 slots live.
All inputs are finite; a program needn't handle non-finite values.
Results may differ from the reference program's by a relative error of at most 0.019.
Values may be sent and summed in bfloat16 or wider, within the bound.
No kernel may reach another device: no remote copies, remote signals or barrier semaphores. Data moves between devices by JAX's collectives and lax.ppermute only.
A program may use at most 32 MiB of HBM per device.

```python
import jax
import jax.numpy as jnp
from jax import lax

C = 256
P_SIZE = 128
SPECIES = 4
EMAX = 512
TMAX = 1024
NX = 128
NY = 16


def tile_counts(key, most):
    counts = jax.random.randint(key, (NX, NY), most // 4, most + 1)
    return counts.at[0, 0].set(most)


def edge_counts(key):
    return tile_counts(jax.random.fold_in(key, 11), EMAX)


def draw_edge_count(key, part):
    return edge_counts(key).astype(jnp.int32)


def draw_trip_count(key, part):
    return tile_counts(jax.random.fold_in(key, 12), TMAX).astype(jnp.int32)


def draw_edge_index(key, part):
    key = jax.random.fold_in(key, 3)
    first, second = jax.random.split(key)
    centre = jax.random.randint(first, (NX, NY, 1, EMAX), 0, P_SIZE)
    code = jax.random.randint(second, (NX, NY, 1, EMAX), 0, 9 * P_SIZE)
    return jnp.concatenate([centre, code], axis=2).astype(jnp.int32)


def draw_trip_index(key, part):
    counts = edge_counts(key)[:, :, None, None]
    key = jax.random.fold_in(key, 4)
    first, second = jax.random.split(key)
    recv = jax.random.randint(first, (NX, NY, 1, TMAX), 0, counts)
    offset = jax.random.randint(second, (NX, NY, 1, TMAX), 0, counts - 1)
    partner = (recv + 1 + offset) % counts
    return jnp.concatenate([recv, partner], axis=2).astype(jnp.int32)


def plant(values, own_key, smallest, largest):
    longest = values.shape.index(max(values.shape))
    spots = []
    for shift in (0, 1):
        where = [jax.random.randint(jax.random.fold_in(own_key, axis), (), 0, length) for axis, length in enumerate(values.shape)]
        where[longest] = (where[longest] + shift) % values.shape[longest]
        spots.append(tuple(where))
    return values.at[spots[0]].set(smallest).at[spots[1]].set(largest)


def steps_of(key, dims, pieces, low, high):
    gain, own = 1.0, jax.random.fold_in(key, 6)
    for axis_at, blocks in pieces:
        steps = jnp.exp(jax.random.uniform(jax.random.fold_in(own, axis_at), (blocks,), jnp.float32, low / len(pieces), high / len(pieces)))
        gain = gain * jnp.repeat(steps, dims[axis_at] // blocks).reshape([-1 if axis == axis_at else 1 for axis in range(len(dims))])
    return gain


def gaussian(stream_key, extent, width, reach, shards=(), kind=jnp.bfloat16):
    array = jax.random.normal(stream_key, extent, jnp.float32) * width
    if len(shards) > 0:
        array = steps_of(stream_key, extent, shards, -0.22, 0.18) * array
    return jnp.clip(array, min=-reach, max=reach).astype(kind)


def setup_inputs(seed: int = 0) -> dict:
    key_list = jax.random.split(jax.random.key(seed), 16)
    return {
        "state": gaussian(key_list[0], (NX, NY, P_SIZE, C), 1.0, 6.0, ((0, 64), (1, 16))),
        "species": plant(jax.random.randint(key_list[1], (NX, NY, P_SIZE), 0, SPECIES), jax.random.fold_in(key_list[1], 1), 0, SPECIES - 1).astype(jnp.int32),
        "species_bias": gaussian(key_list[2], (SPECIES, C), 1.0, 4.0, (), jnp.float32),
        "edge_index": draw_edge_index(jax.random.fold_in(key_list[15], 71), 0),
        "edge_count": draw_edge_count(jax.random.fold_in(key_list[15], 71), 0),
        "edge_dist": jnp.clip(0.2 + 0.7 * jax.random.uniform(key_list[5], (NX, NY, EMAX), jnp.float32) ** steps_of(key_list[5], (NX, NY, EMAX), ((0, 64), (1, 16)), -0.2, 0.2), 0.2, 0.9),
        "trip_index": draw_trip_index(jax.random.fold_in(key_list[15], 71), 0),
        "trip_count": draw_trip_count(jax.random.fold_in(key_list[15], 71), 0),
        "trip_cos": jnp.clip(jax.random.uniform(key_list[8], (NX, NY, TMAX), jnp.float32, -1.0, 1.0) * steps_of(key_list[8], (NX, NY, TMAX), ((0, 64), (1, 16)), -0.4, 0.0), -1.0, 1.0),
        "radial_weight": gaussian(key_list[9], (C,), 1.0, 4.0, (), jnp.float32),
        "norm_gain": jnp.clip(1.0 + 0.18 * jax.random.normal(key_list[10], (C,), jnp.float32), 0.1, 1.9),
        "w_centre": gaussian(key_list[11], (C, C), C ** -0.5, 0.375),
        "w_neigh": gaussian(key_list[12], (C, C), C ** -0.5, 0.375),
        "w_mix": gaussian(key_list[13], (C, C), C ** -0.5, 0.375),
        "w_out": gaussian(key_list[14], (C, C), C ** -0.5, 0.375),
    }


def reference(state, species, species_bias, edge_index, edge_count, edge_dist, trip_index, trip_count, trip_cos, radial_weight, norm_gain, w_centre, w_neigh, w_mix, w_out):
    flat = state.reshape(-1, C)
    proj_a = jnp.dot(flat, w_centre, preferred_element_type=jnp.float32) + species_bias[species.reshape(-1)]
    proj_a = proj_a.reshape(NX, NY * P_SIZE, C)
    proj_b = jnp.dot(flat, w_neigh, preferred_element_type=jnp.float32).astype(jnp.bfloat16).reshape(NX, NY * P_SIZE, C)
    columns = jnp.arange(NY, dtype=jnp.int32)[:, None]
    slots_e = jnp.arange(EMAX, dtype=jnp.int32)[None, :]
    slots_t = jnp.arange(TMAX, dtype=jnp.int32)[None, :]

    def row_step(agg, ix):
        rows = (ix + jnp.arange(3, dtype=jnp.int32) - 1) % NX
        nearby = proj_b[rows].reshape(3 * NY * P_SIZE, C)
        centre = edge_index[ix, :, 0, :]
        code = edge_index[ix, :, 1, :]
        cell = code // P_SIZE
        neighbour = cell // 3 * (NY * P_SIZE) + (columns + cell % 3 - 1) % NY * P_SIZE + code % P_SIZE
        centre_flat = columns * P_SIZE + centre
        valid = slots_e < edge_count[ix][:, None]
        dist = edge_dist[ix]
        pre = proj_a[ix][centre_flat] + nearby[neighbour].astype(jnp.float32) + dist[..., None] * radial_weight
        envelope = (1.0 - dist * dist) ** 2
        feat = jnp.where(valid[..., None], jax.nn.silu(pre) * envelope[..., None], 0.0).astype(jnp.bfloat16)
        mixed = jnp.dot(feat.reshape(-1, C), w_mix, preferred_element_type=jnp.float32).astype(jnp.bfloat16).reshape(NY, EMAX, C)
        recv = trip_index[ix, :, 0, :]
        partner = trip_index[ix, :, 1, :]
        weight = jnp.where(slots_t < trip_count[ix][:, None], trip_cos[ix], 0.0)
        left = jax.vmap(lambda table, idx: table[idx])(feat, recv).astype(jnp.float32)
        right = jax.vmap(lambda table, idx: table[idx])(mixed, partner).astype(jnp.float32)
        message = weight[..., None] * left * right
        edge_msg = jnp.zeros((NY, EMAX, C), jnp.float32).at[columns, recv].add(message)
        partial_sum = jnp.zeros((3 * NY * P_SIZE, C), jnp.float32).at[neighbour.reshape(-1)].add(edge_msg.reshape(-1, C))
        partial_sum = partial_sum.reshape(3, NY * P_SIZE, C)
        for k in range(3):
            agg = agg.at[rows[k]].add(partial_sum[k])
        return (agg, None)
    agg = jnp.zeros((NX, NY * P_SIZE, C), jnp.float32)
    agg, _ = lax.scan(row_step, agg, jnp.arange(NX, dtype=jnp.int32))
    agg = agg.reshape(-1, C)
    scale = lax.rsqrt(lax.optimization_barrier(jnp.mean(agg * agg, axis=-1, keepdims=True)) + 1e-05)
    normed = (agg * scale * norm_gain).astype(jnp.bfloat16)
    updated = flat.astype(jnp.float32) + jnp.dot(normed, w_out, preferred_element_type=jnp.float32)
    return updated.astype(jnp.bfloat16).reshape(NX, NY, P_SIZE, C)
```

```python
import jax
import jax.numpy as jnp
from jax import lax
from jax.experimental import pallas as pl
from jax.experimental.pallas import tpu as pltpu
from jax.sharding import PartitionSpec as P


F32 = jnp.float32
BF16 = jnp.bfloat16
NT = (((1,), (1,)), ((), ()))
TN = (((0,), (0,)), ((), ()))
VMEM_LIMIT = 32 * 1024 * 1024


def core_bit():
    return lax.rem(lax.axis_index("gy"), 2)


def dot(left, right, dims=(((1,), (0,)), ((), ()))):
    return lax.dot_general(left, right, dims, preferred_element_type=F32)


def onehot(index, first, count):
    rows = lax.broadcasted_iota(jnp.int32, (count, index.shape[1]), 0) + first
    return jnp.where(rows == index, 1.0, 0.0).astype(BF16)


def near_codes(pack_ref, holder, core, edges, atoms):
    code = pack_ref[holder, core, 3:4, edges : 2 * edges].astype(jnp.int32)
    slot = jnp.bitwise_and(code, atoms - 1)
    return jnp.where(core == 1, 8 * atoms + 2 * slot - code, code)


def pack_kernel(count_e, count_t, index_e, dist, index_t, cosine, species, out):
    edges = dist.shape[2]
    trips = cosine.shape[2]
    atoms = species.shape[2]
    out[...] = jnp.zeros(out.shape, F32)
    lanes_e = lax.broadcasted_iota(jnp.int32, (1, edges), 1)
    lanes_t = lax.broadcasted_iota(jnp.int32, (1, trips), 1)
    for row in range(2):
        out[row, 0:2, :] = index_t[row, 0].astype(F32)
        out[row, 2:3, :] = jnp.where(lanes_t < count_t[row, 0], cosine[row], 0.0)
        out[row, 3:4, 0:edges] = index_e[row, 0, 0:1, :].astype(F32)
        out[row, 3:4, edges : 2 * edges] = index_e[row, 0, 1:2, :].astype(F32)
        reach = dist[row]
        envelope = (1.0 - reach * reach) ** 2
        out[row, 4:5, 0:edges] = reach
        out[row, 4:5, edges : 2 * edges] = jnp.where(lanes_e < count_e[row, 0], envelope, 0.0)
        out[row, 5:6, 0:atoms] = species[row].astype(F32)


def prep_kernel(
    pack, own, edge_col, pair_own, pair_edge, w_neigh, w_centre, bias, radial, links, pre, rows128
):
    core = core_bit()
    far = 1 - core
    edges = links.shape[1]
    trips = pack.shape[3]
    atoms = own.shape[2]
    kinds = bias.shape[0]
    for tile in range(2):
        holder = core if tile == 0 else far
        recv = pack[holder, core, 0:1, :].astype(jnp.int32)
        partner = pack[holder, core, 1:2, :].astype(jnp.int32)
        weight = pack[holder, core, 2:3, :]
        into = onehot(recv, 0, edges)
        rows = lax.broadcasted_iota(jnp.int32, (edges, trips), 0)
        out_of = jnp.where(rows == partner, weight, 0.0).astype(BF16)
        links[tile] = dot(out_of, into, NT).astype(BF16)
    rows128[...] = jnp.zeros(rows128.shape, F32)
    rows128[0:kinds, :] = bias[...]
    rows128[kinds : kinds + 1, :] = radial[...]
    columns = jnp.transpose(rows128[...])
    neigh_t = jnp.transpose(w_neigh[...])
    centre_t = jnp.transpose(w_centre[...])

    def row_states(row):
        return [edge_col[row, 0], own[row, 0], pair_own[far, row, 0], pair_edge[far, row, 0]]

    mine = row_states(core)
    other = row_states(far)
    near = []
    for states in (mine, other):
        stacked = jnp.concatenate(states, axis=0)
        near.append(dot(neigh_t, stacked, NT).astype(BF16))
    for tile in range(2):
        holder = core if tile == 0 else far
        kind = pack[holder, core, 5:6, 0:atoms]
        proj = dot(centre_t, mine[1 + tile], NT)
        for s in range(kinds):
            proj = proj + jnp.where(kind == float(s), columns[:, s : s + 1], 0.0)
        upper = proj.astype(BF16)
        lower = (proj - upper.astype(F32)).astype(BF16)
        span = slice(tile * atoms, (tile + 3) * atoms)
        values = jnp.concatenate([near[0][:, span], near[1][:, span], upper, lower], axis=1)
        code = near_codes(pack, holder, core, edges, atoms)
        centre = pack[holder, core, 3:4, 0:edges].astype(jnp.int32)
        pick_centre = onehot(centre, 0, atoms)
        picks = jnp.concatenate(
            [onehot(code, 3 * atoms, 6 * atoms), pick_centre, pick_centre], axis=0
        )
        reach = pack[holder, core, 4:5, 0:edges]
        pre[tile] = dot(values, picks) + columns[:, kinds : kinds + 1] * reach


def edge_kernel(
    pack,
    links,
    pre,
    remote_own,
    remote_edge,
    w_neigh,
    w_mix,
    post,
    side,
    owned,
    remote_out,
    corner_near,
    corner_far,
):
    core = core_bit()
    far = 1 - core
    edges = links.shape[1]
    atoms = remote_own.shape[1]
    neigh_t = jnp.transpose(w_neigh[...])
    mix_t = jnp.transpose(w_mix[...])
    stacked = jnp.concatenate(
        [remote_edge[core], remote_own[core], remote_own[far], remote_edge[far]], axis=0
    )
    near = dot(neigh_t, stacked, NT).astype(BF16)
    spreads = []
    for tile in range(2):
        holder = core if tile == 0 else far
        code = near_codes(pack, holder, core, edges, atoms)
        envelope = pack[holder, core, 4:5, edges : 2 * edges]
        pick = onehot(code, 0, 9 * atoms)
        total = pre[tile] + dot(near[:, tile * atoms : (tile + 3) * atoms], pick[0 : 3 * atoms])
        feat = (0.5 * total * (1.0 + jnp.tanh(0.5 * total)) * envelope).astype(BF16)
        mixed = dot(mix_t, feat).astype(BF16)
        message = (feat.astype(F32) * dot(mixed, links[tile])).astype(BF16)
        spreads.append(dot(pick, message, NT))

    def cell(row, slot):
        total = None
        for tile in range(2):
            if 0 <= slot - tile < 3:
                at = (3 * row + slot - tile) * atoms
                part = spreads[tile][at : at + atoms]
                total = part if total is None else total + part
        return total

    corner_near[...] = cell(0, 0).astype(BF16)
    corner_far[...] = cell(0, 3).astype(BF16)
    remote_out[core] = cell(0, 1).astype(BF16)
    remote_out[far] = cell(0, 2).astype(BF16)
    for row, at in ((1, core), (2, far)):
        side[at] = cell(row, 0).astype(BF16)
        owned[at] = cell(row, 1)
        post[0, at] = cell(row, 2).astype(BF16)
        post[1, at] = cell(row, 3).astype(BF16)


def side_kernel(side, posts, out):
    far = 1 - core_bit()
    out[...] = (side[...].astype(F32) + posts[far, 1].astype(F32)).astype(BF16)


def final_kernel(
    state, owned, posts, remote, remotes, corner_near, corner_far, side, gain, w_out, out
):
    core = core_bit()
    far = 1 - core
    for row, extra, corner in (
        (core, remote[core], corner_near[...]),
        (far, remotes[far, core], corner_far[...]),
    ):
        total = owned[row] + posts[far, 0, row].astype(F32) + side[row].astype(F32)
        total = total + extra.astype(F32) + corner.astype(F32)
        scale = lax.rsqrt(jnp.mean(total * total, axis=-1, keepdims=True) + 1e-05)
        normed = (total * scale * gain[...]).astype(BF16)
        out[row, 0] = (state[row, 0].astype(F32) + dot(normed, w_out[...])).astype(BF16)


VMEM = pl.BlockSpec(memory_space=pltpu.VMEM)
SMEM = pl.BlockSpec(memory_space=pltpu.SMEM)


def call(kernel, outs, *operands, scratch=(), scalars=0):
    return pl.pallas_call(
        kernel,
        out_shape=outs,
        in_specs=[SMEM] * scalars + [VMEM] * (len(operands) - scalars),
        out_specs=jax.tree.map(lambda _: VMEM, outs),
        scratch_shapes=list(scratch),
        compiler_params=pltpu.CompilerParams(vmem_limit_bytes=VMEM_LIMIT),
    )(*operands)


def pairings():
    count_x, count_y = lax.axis_size("gx"), lax.axis_size("gy")

    def at(x, y):
        return (x % count_x) * count_y + y % count_y

    along_y = []
    along_x, near, far = [], [], []
    for y in range(0, count_y, 2):
        first, second = (y + 2) % count_y, y + 1
        along_y += [(first, second), (second, first)]
    for x in range(count_x):
        for y in range(0, count_y, 2):
            first, second = at(x + 1, y), at(x, y + 1)
            along_x += [(first, second), (second, first)]
            first, second = at(x + 1, y + 2), at(x, y + 1)
            near += [(first, second), (second, first)]
            far += [(at(x, y), at(x - 1, y + 2)), (at(x, y + 1), at(x + 1, y - 1))]
    chips = [[y, y + 1] for y in range(0, count_y, 2)]
    return along_y, along_x, near, far, chips


def body(
    state,
    species,
    species_bias,
    edge_index,
    edge_count,
    edge_dist,
    trip_index,
    trip_count,
    trip_cos,
    radial_weight,
    norm_gain,
    w_centre,
    w_neigh,
    w_mix,
    w_out,
):
    size_x, _, atoms, chans = state.shape
    edges = edge_index.shape[3]
    trips = trip_index.shape[3]
    along_y, along_x, near, far, chips = pairings()
    both = ("gx", "gy")
    core = core_bit()

    def gathered(value):
        return lax.all_gather(value, "gy", axis_index_groups=chips)

    def shaped(*shape, dtype=BF16):
        return jax.ShapeDtypeStruct(shape, dtype)

    def worked_row(pair):
        return lax.dynamic_index_in_dim(pair, core, axis=1, keepdims=False)[:, 0]

    edge_col = lax.ppermute(state, "gy", along_y)
    pair_own = gathered(state)
    remote_own = lax.ppermute(worked_row(pair_own), both, along_x)
    pair_edge = gathered(edge_col)
    remote_edge = lax.ppermute(worked_row(pair_edge), both, along_x)
    packed = call(
        pack_kernel,
        shaped(size_x, 8, trips, dtype=F32),
        edge_count,
        trip_count,
        edge_index,
        edge_dist,
        trip_index,
        trip_cos,
        species,
        scalars=2,
    )
    pack = gathered(packed)
    links, pre = call(
        prep_kernel,
        (shaped(2, edges, edges), shaped(2, chans, edges, dtype=F32)),
        pack,
        state,
        edge_col,
        pair_own,
        pair_edge,
        w_neigh,
        w_centre,
        species_bias,
        radial_weight.reshape(1, chans),
        scratch=[pltpu.VMEM((128, chans), F32)],
    )
    tile = (atoms, chans)
    post, side, owned, remote_out, corner_near, corner_far = call(
        edge_kernel,
        (
            shaped(2, 2, *tile),
            shaped(2, *tile),
            shaped(2, *tile, dtype=F32),
            shaped(2, *tile),
            shaped(*tile),
            shaped(*tile),
        ),
        pack,
        links,
        pre,
        remote_own,
        remote_edge,
        w_neigh,
        w_mix,
    )
    posts = gathered(post)
    side_in = lax.ppermute(call(side_kernel, shaped(2, *tile), side, posts), "gy", along_y)
    remote_in = lax.ppermute(remote_out, both, along_x)
    near_in = lax.ppermute(corner_near, both, near)
    far_in = lax.ppermute(corner_far, both, far)
    remotes = gathered(remote_in)
    return call(
        final_kernel,
        shaped(*state.shape),
        state,
        owned,
        posts,
        remote_in,
        remotes,
        near_in,
        far_in,
        side_in,
        norm_gain.reshape(1, chans),
        w_out,
    )


def solution(mesh):
    placed = (
        P("gx", "gy", None, None),
        P("gx", "gy", None),
        P(),
        P("gx", "gy", None, None),
        P("gx", "gy"),
        P("gx", "gy", None),
        P("gx", "gy", None, None),
        P("gx", "gy"),
        P("gx", "gy", None),
        P(),
        P(),
        P(),
        P(),
        P(),
        P(),
    )
    return jax.shard_map(
        body, mesh=mesh, in_specs=placed, out_specs=P("gx", "gy", None, None), check_vma=False
    )
```

```python
import functools

import jax
import jax.numpy as jnp
from jax import lax
from jax.experimental import pallas as pl
from jax.experimental.pallas import tpu as pltpu
from jax.sharding import PartitionSpec as P


F32 = jnp.float32
BF16 = jnp.bfloat16
NT = (((1,), (1,)), ((), ()))
TN = (((0,), (0,)), ((), ()))
VMEM_LIMIT = 32 * 1024 * 1024
VMEM_ALL = 63 * 1024 * 1024
LINES = 32


def core_bit():
    return lax.rem(lax.axis_index("gy"), 2)


def dot(left, right, dims=(((1,), (0,)), ((), ()))):
    return lax.dot_general(left, right, dims, preferred_element_type=F32)


def onehot(index, first, count):
    rows = lax.broadcasted_iota(jnp.int32, (count, index.shape[1]), 0) + first
    return jnp.where(rows == index, 1.0, 0.0).astype(BF16)


def fields(block, edges, trips, atoms, core):
    lines = block.astype(F32)
    width = lines.shape[1]
    at = 0

    def take(length):
        nonlocal at
        count = length // width
        parts = [lines[at + i : at + i + 1] for i in range(count)]
        at += count
        return jnp.concatenate(parts, axis=1)

    half = float(edges // 2)
    recv = (take(trips) + half).astype(jnp.int32)
    partner = (take(trips) + half).astype(jnp.int32)
    weight = take(trips)
    centre = take(edges).astype(jnp.int32)
    cell = take(edges)
    cell = jnp.where(core == 1, 8.0 - cell, cell)
    code = (cell * float(atoms) + take(edges)).astype(jnp.int32)
    reach = take(edges)
    reach = reach + take(edges)
    kind = lines[at : at + 1, 0:atoms]
    return recv, partner, weight, centre, code, reach, kind


def pack_kernel(
    count_e_hbm,
    count_t_hbm,
    state_hbm,
    index_e_hbm,
    dist_hbm,
    index_t_hbm,
    cosine_hbm,
    species_hbm,
    out,
    lines,
    count_e,
    count_t,
    index_e,
    dist,
    index_t,
    cosine,
    species,
    sems,
):
    edges = dist.shape[2]
    trips = cosine.shape[2]
    atoms = species.shape[2]
    width = lines.shape[1]
    half = edges // 2
    copies = [
        (count_e_hbm, count_e),
        (count_t_hbm, count_t),
        (index_e_hbm, index_e),
        (dist_hbm, dist),
        (index_t_hbm, index_t),
        (cosine_hbm, cosine),
        (species_hbm, species),
    ]
    copies += [(state_hbm.at[row, 0], out.at[row, pl.ds(0, atoms)]) for row in range(2)]
    copies = [
        pltpu.make_async_copy(source, target, sems.at[i])
        for i, (source, target) in enumerate(copies)
    ]
    for copy in copies:
        copy.start()
    lanes_e = lax.broadcasted_iota(jnp.int32, (1, edges), 1)
    lanes_t = lax.broadcasted_iota(jnp.int32, (1, trips), 1)
    for copy in copies:
        copy.wait()
    for row in range(2):
        at = 0

        def put(values):
            nonlocal at
            for first in range(0, values.shape[1], width):
                lines[at : at + 1, :] = values[:, first : first + width]
                at += 1

        lines[...] = jnp.zeros(lines.shape, F32)
        put((index_t[row, 0, 0:1, :] - half).astype(F32))
        put((index_t[row, 0, 1:2, :] - half).astype(F32))
        put(jnp.where(lanes_t < count_t[row], cosine[row], 0.0))
        put(index_e[row, 0, 0:1, :].astype(F32))
        code = index_e[row, 0, 1:2, :].astype(F32)
        cell = jnp.floor(code * (1.0 / atoms))
        put(cell)
        put(code - cell * float(atoms))
        reach = jnp.where(lanes_e < count_e[row], dist[row], 1.0)
        upper = reach.astype(BF16).astype(F32)
        put(upper)
        put(reach - upper)
        lines[at : at + 1, 0:atoms] = species[row].astype(F32)
        out[row, atoms : atoms + LINES] = lines[...].astype(BF16)


def link_matrix(recv, partner, weight, edges):
    into = onehot(recv, 0, edges)
    rows = lax.broadcasted_iota(jnp.int32, (edges, recv.shape[1]), 0)
    out_of = jnp.where(rows == partner, weight, 0.0).astype(BF16)
    return dot(out_of, into, NT).astype(BF16)


def scalar_columns(rows128, bias, radial):
    kinds = bias.shape[0]
    rows128[...] = jnp.zeros(rows128.shape, F32)
    rows128[0:kinds, :] = bias[...]
    rows128[kinds : kinds + 1, :] = radial[...]
    return jnp.transpose(rows128[...])


def centre_split(centre_t, states, kind, columns, kinds):
    proj = dot(centre_t, states, NT)
    for s in range(kinds):
        proj = proj + jnp.where(kind == float(s), columns[:, s : s + 1], 0.0)
    upper = proj.astype(BF16)
    return upper, (proj - upper.astype(F32)).astype(BF16)


def mine_kernel(
    trips,
    pack,
    edge_col,
    pair_edge,
    w_neigh,
    w_centre,
    w_out,
    gain,
    bias,
    radial,
    links,
    pre,
    near,
    w_out_kept,
    gain_kept,
    rows128,
):
    w_out_kept[...] = w_out[...]
    gain_kept[...] = gain[...]
    core = core_bit()
    far = 1 - core
    edges = links.shape[1]
    atoms = edge_col.shape[2]
    kinds = bias.shape[0]
    columns = scalar_columns(rows128, bias, radial)
    neigh_t = jnp.transpose(w_neigh[...])
    centre_t = jnp.transpose(w_centre[...])

    def row_states(row):
        return [
            edge_col[row, 0],
            pack[core, row, 0:atoms],
            pack[far, row, 0:atoms],
            pair_edge[far, row, 0],
        ]

    mine = row_states(core)
    rows = [
        dot(neigh_t, jnp.concatenate(states, axis=0), NT).astype(BF16)
        for states in (mine, row_states(far))
    ]
    near[...] = rows[0]
    for tile in range(2):
        holder = core if tile == 0 else far
        recv, partner, weight, centre, code, reach, kind = fields(
            pack[holder, core, atoms:], edges, trips, atoms, core
        )
        links[tile] = link_matrix(recv, partner, weight, edges)
        upper, lower = centre_split(centre_t, mine[1 + tile], kind, columns, kinds)
        span = slice(tile * atoms, (tile + 3) * atoms)
        values = jnp.concatenate([rows[0][:, span], rows[1][:, span], upper, lower], axis=1)
        pick_centre = onehot(centre, 0, atoms)
        picks = jnp.concatenate(
            [onehot(code, 3 * atoms, 6 * atoms), pick_centre, pick_centre], axis=0
        )
        pre[tile] = dot(values, picks) + columns[:, kinds : kinds + 1] * reach


def remote_kernel(trips, remote, w_centre, bias, radial, links, pre, rows128):
    core = core_bit()
    far = 1 - core
    edges = links.shape[1]
    atoms = remote.shape[2] - LINES
    kinds = bias.shape[0]
    columns = scalar_columns(rows128, bias, radial)
    centre_t = jnp.transpose(w_centre[...])
    for tile in range(2):
        holder = core if tile == 0 else far
        recv, partner, weight, centre, _, reach, kind = fields(
            remote[holder, far, atoms:], edges, trips, atoms, core
        )
        links[tile] = link_matrix(recv, partner, weight, edges)
        states = remote[holder, far, 0:atoms]
        values = jnp.concatenate(centre_split(centre_t, states, kind, columns, kinds), axis=1)
        pick_centre = onehot(centre, 0, atoms)
        picks = jnp.concatenate([pick_centre, pick_centre], axis=0)
        pre[tile] = dot(values, picks) + columns[:, kinds : kinds + 1] * reach


def edge_kernel(
    trips,
    pack,
    remote,
    remote_edge,
    links_mine,
    pre_mine,
    near_mine,
    links_remote,
    pre_remote,
    w_neigh,
    w_mix,
    post,
    side,
    owned,
):
    core = core_bit()
    far = 1 - core
    edges = links_mine.shape[1]
    atoms = owned.shape[1]
    neigh_t = jnp.transpose(w_neigh[...])
    mix_t = jnp.transpose(w_mix[...])

    def remote_row(row):
        states = [
            remote_edge[core, row, 0],
            remote[core, row, 0:atoms],
            remote[far, row, 0:atoms],
            remote_edge[far, row, 0],
        ]
        return dot(neigh_t, jnp.concatenate(states, axis=0), NT).astype(BF16)

    near_next = remote_row(far)
    near_last = remote_row(core)
    near_own = near_mine[...]
    spreads = []
    for source, row, links, pre, nears, kept in (
        (pack, core, links_mine, pre_mine, (near_next,), 3),
        (remote, far, links_remote, pre_remote, (near_last, near_next, near_own), 6),
    ):
        for tile in range(2):
            holder = core if tile == 0 else far
            _, _, _, _, code, reach, _ = fields(
                source[holder, row, atoms:], edges, trips, atoms, core
            )
            pick = onehot(code, 0, 9 * atoms)
            span = slice(tile * atoms, (tile + 3) * atoms)
            values = jnp.concatenate([near[:, span] for near in nears], axis=1)
            total = pre[tile] + dot(values, pick[0 : values.shape[1]])
            envelope = (1.0 - reach * reach) ** 2
            feat = (0.5 * total * (1.0 + jnp.tanh(0.5 * total)) * envelope).astype(BF16)
            mixed = dot(mix_t, feat).astype(BF16)
            message = (feat.astype(F32) * dot(mixed, links[tile])).astype(BF16)
            spreads.append(dot(pick[kept * atoms :], message, NT))

    def cell(row, slot):
        total = None
        for tile in range(2):
            if 0 <= slot - tile < 3:
                parts = [spreads[tile][(3 * row + slot - tile) * atoms :][:atoms]]
                if row == 0:
                    parts.append(spreads[2 + tile][(slot - tile) * atoms :][:atoms])
                for part in parts:
                    total = part if total is None else total + part
        return total

    for row, at in ((0, core), (1, far)):
        side[at] = cell(row, 0).astype(BF16)
        owned[at] = cell(row, 1)
        post[0, at] = cell(row, 2).astype(BF16)
        post[1, at] = cell(row, 3).astype(BF16)


def side_kernel(side, posts, out):
    far = 1 - core_bit()
    out[...] = (side[...].astype(F32) + posts[far, 1].astype(F32)).astype(BF16)


def final_kernel(pack, owned, posts, side, gain, w_out, out):
    core = core_bit()
    far = 1 - core
    atoms = owned.shape[1]
    for row in range(2):
        total = owned[row] + posts[far, 0, row].astype(F32) + side[row].astype(F32)
        scale = lax.rsqrt(jnp.mean(total * total, axis=-1, keepdims=True) + 1e-05)
        normed = (total * scale * gain[...]).astype(BF16)
        out[row, 0] = (
            pack[core, row, 0:atoms].astype(F32) + dot(normed, w_out[...])
        ).astype(BF16)


VMEM = pl.BlockSpec(memory_space=pltpu.VMEM)


HBM = pl.BlockSpec(memory_space=pltpu.HBM)


def call(kernel, outs, *operands, scratch=(), specs=None, limit=VMEM_LIMIT):
    return pl.pallas_call(
        kernel,
        out_shape=outs,
        in_specs=specs or [VMEM] * len(operands),
        out_specs=jax.tree.map(lambda _: VMEM, outs),
        scratch_shapes=list(scratch),
        compiler_params=pltpu.CompilerParams(vmem_limit_bytes=limit),
    )(*operands)


def pairings():
    count_x, count_y = lax.axis_size("gx"), lax.axis_size("gy")
    along_y, along_x = [], []
    for y in range(0, count_y, 2):
        first, second = (y + 2) % count_y, y + 1
        along_y += [(first, second), (second, first)]
    for x in range(count_x):
        for y in range(0, count_y, 2):
            first, second = (x + 1) % count_x * count_y + y, x * count_y + y + 1
            along_x += [(first, second), (second, first)]
    chips = [[y, y + 1] for y in range(0, count_y, 2)]
    return along_y, along_x, chips


def body(
    state,
    species,
    species_bias,
    edge_index,
    edge_count,
    edge_dist,
    trip_index,
    trip_count,
    trip_cos,
    radial_weight,
    norm_gain,
    w_centre,
    w_neigh,
    w_mix,
    w_out,
):
    size_x, _, atoms, chans = state.shape
    edges = edge_index.shape[3]
    trips = trip_index.shape[3]
    along_y, along_x, chips = pairings()
    both = ("gx", "gy")

    def gathered(value):
        return lax.all_gather(value, "gy", axis_index_groups=chips)

    def shaped(*shape, dtype=BF16):
        return jax.ShapeDtypeStruct(shape, dtype)

    edge_col = lax.ppermute(state, "gy", along_y)
    packed = call(
        pack_kernel,
        shaped(size_x, atoms + LINES, chans),
        edge_count.reshape(size_x),
        trip_count.reshape(size_x),
        state,
        edge_index,
        edge_dist,
        trip_index,
        trip_cos,
        species,
        specs=[HBM] * 8,
        limit=VMEM_ALL,
        scratch=[
            pltpu.VMEM((LINES, chans), F32),
            pltpu.SMEM((size_x,), jnp.int32),
            pltpu.SMEM((size_x,), jnp.int32),
            *(
                pltpu.VMEM(each.shape, each.dtype)
                for each in (edge_index, edge_dist, trip_index, trip_cos, species)
            ),
            pltpu.SemaphoreType.DMA((9,)),
        ],
    )
    pack = gathered(packed)
    remote = lax.ppermute(pack, both, along_x)
    pair_edge = gathered(edge_col)
    remote_edge = lax.ppermute(pair_edge, both, along_x)
    radial = radial_weight.reshape(1, chans)
    links = shaped(2, edges, edges)
    pre = shaped(2, chans, edges, dtype=F32)
    links_mine, pre_mine, near_mine, w_out, gain = call(
        functools.partial(mine_kernel, trips),
        (
            links,
            pre,
            shaped(chans, 4 * atoms),
            shaped(*w_out.shape),
            shaped(1, chans, dtype=F32),
        ),
        pack,
        edge_col,
        pair_edge,
        w_neigh,
        w_centre,
        w_out,
        norm_gain.reshape(1, chans),
        species_bias,
        radial,
        scratch=[pltpu.VMEM((128, chans), F32)],
    )
    links_remote, pre_remote = call(
        functools.partial(remote_kernel, trips),
        (links, pre),
        remote,
        w_centre,
        species_bias,
        radial,
        scratch=[pltpu.VMEM((128, chans), F32)],
    )
    tile = (atoms, chans)
    post, side, owned = call(
        functools.partial(edge_kernel, trips),
        (shaped(2, 2, *tile), shaped(2, *tile), shaped(2, *tile, dtype=F32)),
        pack,
        remote,
        remote_edge,
        links_mine,
        pre_mine,
        near_mine,
        links_remote,
        pre_remote,
        w_neigh,
        w_mix,
    )
    posts = gathered(post)
    side_in = lax.ppermute(call(side_kernel, shaped(2, *tile), side, posts), "gy", along_y)
    return call(
        final_kernel,
        shaped(*state.shape),
        pack,
        owned,
        posts,
        side_in,
        gain,
        w_out,
    )


def solution(mesh):
    placed = (
        P("gx", "gy", None, None),
        P("gx", "gy", None),
        P(),
        P("gx", "gy", None, None),
        P("gx", "gy"),
        P("gx", "gy", None),
        P("gx", "gy", None, None),
        P("gx", "gy"),
        P("gx", "gy", None),
        P(),
        P(),
        P(),
        P(),
        P(),
        P(),
    )
    return jax.shard_map(
        body, mesh=mesh, in_specs=placed, out_specs=P("gx", "gy", None, None), check_vma=False
    )
```

```python
import functools

import jax
import jax.numpy as jnp
from jax import lax
from jax.experimental import pallas as pl
from jax.experimental.pallas import tpu as pltpu
from jax.sharding import PartitionSpec as P


F32 = jnp.float32
BF16 = jnp.bfloat16
NT = (((1,), (1,)), ((), ()))
TN = (((0,), (0,)), ((), ()))
VMEM_LIMIT = 32 * 1024 * 1024
VMEM_ALL = 63 * 1024 * 1024
LINES = 48


def core_bit():
    return lax.rem(lax.axis_index("gy"), 2)


def dot(left, right, dims=(((1,), (0,)), ((), ()))):
    return lax.dot_general(left, right, dims, preferred_element_type=F32)


def onehot(index, first, count):
    rows = lax.broadcasted_iota(jnp.int32, (count, index.shape[1]), 0) + first
    return jnp.where(rows == index, 1.0, 0.0).astype(BF16)


def blocked_onehot(low, high, blocks, size, values=1.0):
    base = onehot(low, 0, size)
    return jnp.concatenate(
        [base * jnp.where(high == b, values, 0.0).astype(BF16) for b in blocks],
        axis=0,
    )


def fields(block, edges, trips, atoms, core):
    lines = block.astype(F32)
    width = lines.shape[1]
    at = 0

    def take(length):
        nonlocal at
        count = length // width
        parts = [lines[at + i : at + i + 1] for i in range(count)]
        at += count
        return jnp.concatenate(parts, axis=1)

    half = float(edges // 2)
    recv = (take(trips) + half).astype(jnp.int32)
    partner = (take(trips) + half).astype(jnp.int32)
    weight = take(trips)
    centre = take(edges).astype(jnp.int32)
    cell = take(edges)
    cell = jnp.where(core == 1, 8.0 - cell, cell)
    cell = cell.astype(jnp.int32)
    slot = take(edges).astype(jnp.int32)
    reach = take(edges)
    reach = reach + take(edges)
    kind = lines[at : at + 1, 0:atoms]
    return recv, partner, weight, centre, cell, slot, reach, kind, lines[at + 1 :]


def pack_kernel(
    count_e_hbm,
    count_t_hbm,
    state_hbm,
    index_e_hbm,
    dist_hbm,
    index_t_hbm,
    cosine_hbm,
    species_hbm,
    bias_hbm,
    radial_hbm,
    out,
    lines,
    count_e,
    count_t,
    index_e,
    dist,
    index_t,
    cosine,
    species,
    bias,
    radial,
    sems,
):
    edges = dist.shape[2]
    trips = cosine.shape[2]
    atoms = species.shape[2]
    width = lines.shape[1]
    half = edges // 2
    copies = [
        (count_e_hbm, count_e),
        (count_t_hbm, count_t),
        (index_e_hbm, index_e),
        (dist_hbm, dist),
        (index_t_hbm, index_t),
        (cosine_hbm, cosine),
        (species_hbm, species),
        (bias_hbm, bias),
        (radial_hbm, radial),
    ]
    copies += [(state_hbm.at[row, 0], out.at[row, pl.ds(0, atoms)]) for row in range(2)]
    copies = [
        pltpu.make_async_copy(source, target, sems.at[i])
        for i, (source, target) in enumerate(copies)
    ]
    for copy in copies:
        copy.start()
    lanes_e = lax.broadcasted_iota(jnp.int32, (1, edges), 1)
    lanes_t = lax.broadcasted_iota(jnp.int32, (1, trips), 1)
    for copy in copies:
        copy.wait()
    for row in range(2):
        at = 0

        def put(values):
            nonlocal at
            for first in range(0, values.shape[1], width):
                lines[at : at + 1, :] = values[:, first : first + width]
                at += 1

        lines[...] = jnp.zeros(lines.shape, F32)
        put((index_t[row, 0, 0:1, :] - half).astype(F32))
        put((index_t[row, 0, 1:2, :] - half).astype(F32))
        put(jnp.where(lanes_t < count_t[row], cosine[row], 0.0))
        put(index_e[row, 0, 0:1, :].astype(F32))
        code = index_e[row, 0, 1:2, :].astype(F32)
        cell = jnp.floor(code * (1.0 / atoms))
        put(cell)
        put(code - cell * float(atoms))
        reach = jnp.where(lanes_e < count_e[row], dist[row], 1.0)
        upper = reach.astype(BF16).astype(F32)
        put(upper)
        put(reach - upper)
        lines[at : at + 1, 0:atoms] = species[row].astype(F32)
        at += 1
        for values in (bias[...], radial[...]):
            upper = values.astype(BF16).astype(F32)
            for each in (upper, values - upper):
                lines[at : at + values.shape[0], :] = each
                at += values.shape[0]
        out[row, atoms : atoms + LINES] = lines[...].astype(BF16)


def link_matrix(recv, partner, weight, edges, atoms):
    blocks = range(edges // atoms)

    def parts(index):
        high = lax.div(index, atoms)
        return index - high * atoms, high

    into = blocked_onehot(*parts(recv), blocks, atoms)
    out_of = blocked_onehot(*parts(partner), blocks, atoms, weight)
    return dot(out_of, into, NT).astype(BF16)


def scalar_columns(rows128, lines, kinds):
    bias = lines[0:kinds] + lines[kinds : 2 * kinds]
    radial = lines[2 * kinds : 2 * kinds + 1] + lines[2 * kinds + 1 : 2 * kinds + 2]
    rows128[...] = jnp.zeros(rows128.shape, F32)
    rows128[0:kinds, :] = bias
    rows128[kinds : kinds + 1, :] = radial
    return jnp.transpose(rows128[...])


def centre_split(centre_t, states, kind, columns, kinds):
    proj = dot(centre_t, states, NT)
    for s in range(kinds):
        proj = proj + jnp.where(kind == float(s), columns[:, s : s + 1], 0.0)
    upper = proj.astype(BF16)
    return upper, (proj - upper.astype(F32)).astype(BF16)


def mine_kernel(
    trips,
    kinds,
    pack,
    edge_col,
    pair_edge,
    w_neigh,
    w_centre,
    w_out,
    gain,
    links,
    pre,
    near,
    w_out_kept,
    gain_kept,
    rows128,
):
    w_out_kept[...] = w_out[...]
    gain_kept[...] = gain[...]
    core = core_bit()
    far = 1 - core
    edges = links.shape[1]
    atoms = edge_col.shape[2]
    scalars = fields(pack[core, core, atoms:], edges, trips, atoms, core)[-1]
    columns = scalar_columns(rows128, scalars, kinds)
    neigh_t = jnp.transpose(w_neigh[...])
    centre_t = jnp.transpose(w_centre[...])

    def row_states(row):
        return [
            edge_col[row, 0],
            pack[core, row, 0:atoms],
            pack[far, row, 0:atoms],
            pair_edge[far, row, 0],
        ]

    mine = row_states(core)
    rows = [
        dot(neigh_t, jnp.concatenate(states, axis=0), NT).astype(BF16)
        for states in (mine, row_states(far))
    ]
    near[...] = rows[0]
    for tile in range(2):
        holder = core if tile == 0 else far
        recv, partner, weight, centre, cell, slot, reach, kind, _ = fields(
            pack[holder, core, atoms:], edges, trips, atoms, core
        )
        links[tile] = link_matrix(recv, partner, weight, edges, atoms)
        upper, lower = centre_split(centre_t, mine[1 + tile], kind, columns, kinds)
        span = slice(tile * atoms, (tile + 3) * atoms)
        values = jnp.concatenate([rows[0][:, span], rows[1][:, span], upper, lower], axis=1)
        pick_centre = onehot(centre, 0, atoms)
        picks = jnp.concatenate(
            [blocked_onehot(slot, cell, range(3, 9), atoms), pick_centre, pick_centre], axis=0
        )
        pre[tile] = dot(values, picks) + columns[:, kinds : kinds + 1] * reach


def inner_slots(tile):
    return [slot for slot in (1, 2) if 0 <= slot - tile < 3]


def remote_kernel(
    trips,
    kinds,
    pack,
    remote,
    pre_mine,
    near_mine,
    w_neigh,
    w_centre,
    links,
    pre_mine_out,
    pre,
    rows128,
):
    core = core_bit()
    far = 1 - core
    edges = links.shape[1]
    atoms = remote.shape[2] - LINES
    scalars = fields(remote[core, far, atoms:], edges, trips, atoms, core)[-1]
    columns = scalar_columns(rows128, scalars, kinds)
    neigh_t = jnp.transpose(w_neigh[...])
    centre_t = jnp.transpose(w_centre[...])
    near_last, near_next = [
        dot(
            neigh_t,
            jnp.concatenate([remote[core, row, 0:atoms], remote[far, row, 0:atoms]], axis=0),
            NT,
        ).astype(BF16)
        for row in (core, far)
    ]
    near_own = near_mine[...]
    for tile in range(2):
        holder = core if tile == 0 else far
        recv, partner, weight, centre, cell, slot, reach, kind, _ = fields(
            remote[holder, far, atoms:], edges, trips, atoms, core
        )
        links[tile] = link_matrix(recv, partner, weight, edges, atoms)
        states = remote[holder, far, 0:atoms]
        inner = [at - tile for at in inner_slots(tile)]
        span = slice(tile * atoms, (tile + 3) * atoms)
        values = jnp.concatenate(
            [
                near_last,
                near_next,
                near_own[:, span],
                *centre_split(centre_t, states, kind, columns, kinds),
            ],
            axis=1,
        )
        pick_centre = onehot(centre, 0, atoms)
        blocks = inner + [3 + at for at in inner] + [6, 7, 8]
        picks = jnp.concatenate(
            [blocked_onehot(slot, cell, blocks, atoms), pick_centre, pick_centre], axis=0
        )
        pre[tile] = dot(values, picks) + columns[:, kinds : kinds + 1] * reach
        _, _, _, _, cell, slot, _, _, _ = fields(
            pack[holder, core, atoms:], edges, trips, atoms, core
        )
        picks = blocked_onehot(slot, cell, inner, atoms)
        pre_mine_out[tile] = pre_mine[tile] + dot(near_next, picks)


def edge_kernel(
    trips,
    pack,
    remote,
    remote_edge,
    links_mine,
    pre_mine,
    links_remote,
    pre_remote,
    w_neigh,
    w_mix,
    post,
    side,
    owned,
):
    core = core_bit()
    far = 1 - core
    edges = links_mine.shape[1]
    atoms = owned.shape[1]
    mix_t = jnp.transpose(w_mix[...])
    corners = [remote_edge[core, core, 0], remote_edge[core, far, 0]]
    corners += [remote_edge[far, core, 0], remote_edge[far, far, 0]]
    near = dot(jnp.transpose(w_neigh[...]), jnp.concatenate(corners, axis=0), NT).astype(BF16)
    spreads = []
    for source, row, links, pre, outer, kept in (
        (pack, core, links_mine, pre_mine, (0,), range(3, 9)),
        (remote, far, links_remote, pre_remote, (0, 3), range(6, 9)),
    ):
        for tile in range(2):
            holder = core if tile == 0 else far
            _, _, _, _, cells, slots, reach, _, _ = fields(
                source[holder, row, atoms:], edges, trips, atoms, core
            )
            blocks = [first + 2 * tile for first in outer] + list(kept)
            pick = blocked_onehot(slots, cells, blocks, atoms)
            values = near[:, (2 * tile + 2 - len(outer)) * atoms : (2 * tile + 2) * atoms]
            depth = len(outer) * atoms
            total = pre[tile] + dot(values, pick[0:depth])
            envelope = (1.0 - reach * reach) ** 2
            feat = (0.5 * total * (1.0 + jnp.tanh(0.5 * total)) * envelope).astype(BF16)
            mixed = dot(mix_t, feat).astype(BF16)
            message = (feat.astype(F32) * dot(mixed, links[tile])).astype(BF16)
            spreads.append(dot(pick[depth:], message, NT))

    def cell(row, slot):
        total = None
        for tile in range(2):
            if 0 <= slot - tile < 3:
                parts = [spreads[tile][(3 * row + slot - tile) * atoms :][:atoms]]
                if row == 0:
                    parts.append(spreads[2 + tile][(slot - tile) * atoms :][:atoms])
                for part in parts:
                    total = part if total is None else total + part
        return total

    for row, at in ((0, core), (1, far)):
        side[at] = cell(row, 0).astype(BF16)
        owned[at] = cell(row, 1)
        post[0, at] = cell(row, 2).astype(BF16)
        post[1, at] = cell(row, 3).astype(BF16)


def side_kernel(side, posts, out):
    far = 1 - core_bit()
    out[...] = (side[...].astype(F32) + posts[far, 1].astype(F32)).astype(BF16)


def final_kernel(pack, owned, posts, side, gain, w_out, out):
    core = core_bit()
    far = 1 - core
    atoms = owned.shape[1]
    for row in range(2):
        total = owned[row] + posts[far, 0, row].astype(F32) + side[far, row].astype(F32)
        scale = lax.rsqrt(jnp.mean(total * total, axis=-1, keepdims=True) + 1e-05)
        normed = (total * scale * gain[...]).astype(BF16)
        out[row, 0] = (
            pack[core, row, 0:atoms].astype(F32) + dot(normed, w_out[...])
        ).astype(BF16)


VMEM = pl.BlockSpec(memory_space=pltpu.VMEM)


HBM = pl.BlockSpec(memory_space=pltpu.HBM)


def call(kernel, outs, *operands, scratch=(), specs=None, limit=VMEM_LIMIT):
    return pl.pallas_call(
        kernel,
        out_shape=outs,
        in_specs=specs or [VMEM] * len(operands),
        out_specs=jax.tree.map(lambda _: VMEM, outs),
        scratch_shapes=list(scratch),
        compiler_params=pltpu.CompilerParams(vmem_limit_bytes=limit),
    )(*operands)


def pairings():
    count_x, count_y = lax.axis_size("gx"), lax.axis_size("gy")
    along_y, along_x = [], []
    for y in range(0, count_y, 2):
        first, second = (y + 2) % count_y, y + 1
        along_y += [(first, second), (second, first)]
    for x in range(count_x):
        for y in range(0, count_y, 2):
            first, second = (x + 1) % count_x * count_y + y, x * count_y + y + 1
            along_x += [(first, second), (second, first)]
    chips = [[y, y + 1] for y in range(0, count_y, 2)]
    return along_y, along_x, chips


def body(
    state,
    species,
    species_bias,
    edge_index,
    edge_count,
    edge_dist,
    trip_index,
    trip_count,
    trip_cos,
    radial_weight,
    norm_gain,
    w_centre,
    w_neigh,
    w_mix,
    w_out,
):
    size_x, _, atoms, chans = state.shape
    edges = edge_index.shape[3]
    trips = trip_index.shape[3]
    kinds = species_bias.shape[0]
    along_y, along_x, chips = pairings()
    both = ("gx", "gy")

    def gathered(value):
        return lax.all_gather(value, "gy", axis_index_groups=chips)

    def shaped(*shape, dtype=BF16):
        return jax.ShapeDtypeStruct(shape, dtype)

    edge_col = lax.ppermute(state, "gy", along_y)
    radial = radial_weight.reshape(1, chans)
    packed = call(
        pack_kernel,
        shaped(size_x, atoms + LINES, chans),
        edge_count.reshape(size_x),
        trip_count.reshape(size_x),
        state,
        edge_index,
        edge_dist,
        trip_index,
        trip_cos,
        species,
        species_bias,
        radial,
        specs=[HBM] * 10,
        limit=VMEM_ALL,
        scratch=[
            pltpu.VMEM((LINES, chans), F32),
            pltpu.SMEM((size_x,), jnp.int32),
            pltpu.SMEM((size_x,), jnp.int32),
            *(
                pltpu.VMEM(each.shape, each.dtype)
                for each in (
                    edge_index,
                    edge_dist,
                    trip_index,
                    trip_cos,
                    species,
                    species_bias,
                    radial,
                )
            ),
            pltpu.SemaphoreType.DMA((11,)),
        ],
    )
    pack = gathered(packed)
    remote = lax.ppermute(pack, both, along_x)
    pair_edge = gathered(edge_col)
    remote_edge = lax.ppermute(pair_edge, both, along_x)
    links = shaped(2, edges, edges)
    pre = shaped(2, chans, edges, dtype=F32)
    links_mine, pre_mine, near_mine, w_out, gain = call(
        functools.partial(mine_kernel, trips, kinds),
        (
            links,
            pre,
            shaped(chans, 4 * atoms),
            shaped(*w_out.shape),
            shaped(1, chans, dtype=F32),
        ),
        pack,
        edge_col,
        pair_edge,
        w_neigh,
        w_centre,
        w_out,
        norm_gain.reshape(1, chans),
        scratch=[pltpu.VMEM((128, chans), F32)],
    )
    links_remote, pre_mine, pre_remote = call(
        functools.partial(remote_kernel, trips, kinds),
        (links, pre, pre),
        pack,
        remote,
        pre_mine,
        near_mine,
        w_neigh,
        w_centre,
        scratch=[pltpu.VMEM((128, chans), F32)],
    )
    tile = (atoms, chans)
    post, side, owned = call(
        functools.partial(edge_kernel, trips),
        (shaped(2, 2, *tile), shaped(2, *tile), shaped(2, *tile, dtype=F32)),
        pack,
        remote,
        remote_edge,
        links_mine,
        pre_mine,
        links_remote,
        pre_remote,
        w_neigh,
        w_mix,
    )
    posts = gathered(post)
    side_out = call(side_kernel, shaped(2, *tile), side, posts)
    side_in = lax.all_gather(side_out, "gy", axis_index_groups=[list(pair) for pair in along_y[::2]])
    return call(
        final_kernel,
        shaped(*state.shape),
        pack,
        owned,
        posts,
        side_in,
        gain,
        w_out,
    )


def solution(mesh):
    placed = (
        P("gx", "gy", None, None),
        P("gx", "gy", None),
        P(),
        P("gx", "gy", None, None),
        P("gx", "gy"),
        P("gx", "gy", None),
        P("gx", "gy", None, None),
        P("gx", "gy"),
        P("gx", "gy", None),
        P(),
        P(),
        P(),
        P(),
        P(),
        P(),
    )
    return jax.shard_map(
        body, mesh=mesh, in_specs=placed, out_specs=P("gx", "gy", None, None), check_vma=False
    )
```

```python
import functools

import jax
import jax.numpy as jnp
from jax import lax
from jax.experimental import pallas as pl
from jax.experimental.pallas import tpu as pltpu
from jax.sharding import PartitionSpec as P


F32 = jnp.float32
BF16 = jnp.bfloat16
NT = (((1,), (1,)), ((), ()))
TN = (((0,), (0,)), ((), ()))
VMEM_LIMIT = 32 * 1024 * 1024
VMEM_ALL = 63 * 1024 * 1024
LINES = 48


def core_bit():
    return lax.rem(lax.axis_index("gy"), 2)


def dot(left, right, dims=(((1,), (0,)), ((), ()))):
    return lax.dot_general(left, right, dims, preferred_element_type=F32)


def onehot(index, first, count):
    rows = lax.broadcasted_iota(jnp.int32, (count, index.shape[1]), 0) + first
    return jnp.where(rows == index, 1.0, 0.0).astype(BF16)


def blocked_onehot(low, high, blocks, size, values=1.0):
    base = onehot(low, 0, size)
    return jnp.concatenate(
        [base * jnp.where(high == b, values, 0.0).astype(BF16) for b in blocks],
        axis=0,
    )


def fields(block, edges, trips, atoms, core):
    lines = block.astype(F32)
    width = lines.shape[1]
    at = 0

    def take(length):
        nonlocal at
        count = length // width
        parts = [lines[at + i : at + i + 1] for i in range(count)]
        at += count
        return jnp.concatenate(parts, axis=1)

    half = float(edges // 2)
    recv = (take(trips) + half).astype(jnp.int32)
    partner = (take(trips) + half).astype(jnp.int32)
    weight = take(trips)
    centre = take(edges).astype(jnp.int32)
    cell = take(edges)
    cell = jnp.where(core == 1, 8.0 - cell, cell)
    cell = cell.astype(jnp.int32)
    slot = take(edges).astype(jnp.int32)
    reach = take(edges)
    reach = reach + take(edges)
    kind = lines[at : at + 1, 0:atoms]
    return recv, partner, weight, centre, cell, slot, reach, kind, lines[at + 1 :]


def pack_kernel(
    count_e_hbm,
    count_t_hbm,
    state_hbm,
    index_e_hbm,
    dist_hbm,
    index_t_hbm,
    cosine_hbm,
    species_hbm,
    bias_hbm,
    radial_hbm,
    out,
    lines,
    count_e,
    count_t,
    index_e,
    dist,
    index_t,
    cosine,
    species,
    bias,
    radial,
    sems,
):
    edges = dist.shape[2]
    trips = cosine.shape[2]
    atoms = species.shape[2]
    width = lines.shape[1]
    half = edges // 2
    copies = [
        (count_e_hbm, count_e),
        (count_t_hbm, count_t),
        (index_e_hbm, index_e),
        (dist_hbm, dist),
        (index_t_hbm, index_t),
        (cosine_hbm, cosine),
        (species_hbm, species),
        (bias_hbm, bias),
        (radial_hbm, radial),
    ]
    copies += [(state_hbm.at[row, 0], out.at[row, pl.ds(0, atoms)]) for row in range(2)]
    copies = [
        pltpu.make_async_copy(source, target, sems.at[i])
        for i, (source, target) in enumerate(copies)
    ]
    for copy in copies:
        copy.start()
    lanes_e = lax.broadcasted_iota(jnp.int32, (1, edges), 1)
    lanes_t = lax.broadcasted_iota(jnp.int32, (1, trips), 1)
    lines[...] = jnp.zeros(lines.shape, F32)
    for copy in copies[:-2]:
        copy.wait()
    for row in range(2):
        at = 0

        def put(values):
            nonlocal at
            for first in range(0, values.shape[1], width):
                lines[at : at + 1, :] = values[:, first : first + width]
                at += 1

        put((index_t[row, 0, 0:1, :] - half).astype(F32))
        put((index_t[row, 0, 1:2, :] - half).astype(F32))
        put(jnp.where(lanes_t < count_t[row], cosine[row], 0.0))
        put(index_e[row, 0, 0:1, :].astype(F32))
        code = index_e[row, 0, 1:2, :].astype(F32)
        cell = jnp.floor(code * (1.0 / atoms))
        put(cell)
        put(code - cell * float(atoms))
        reach = jnp.where(lanes_e < count_e[row], dist[row], 1.0)
        upper = reach.astype(BF16).astype(F32)
        put(upper)
        put(reach - upper)
        lines[at : at + 1, 0:atoms] = species[row].astype(F32)
        at += 1
        for values in (bias[...], radial[...]):
            upper = values.astype(BF16).astype(F32)
            for each in (upper, values - upper):
                lines[at : at + values.shape[0], :] = each
                at += values.shape[0]
        out[row, atoms : atoms + LINES] = lines[...].astype(BF16)
    for copy in copies[-2:]:
        copy.wait()


def link_matrix(recv, partner, weight, edges, atoms):
    blocks = range(edges // atoms)

    def parts(index):
        high = lax.div(index, atoms)
        return index - high * atoms, high

    into = blocked_onehot(*parts(recv), blocks, atoms)
    out_of = blocked_onehot(*parts(partner), blocks, atoms, weight)
    return dot(out_of, into, NT).astype(BF16)


def scalar_columns(rows128, lines, kinds):
    bias = lines[0:kinds] + lines[kinds : 2 * kinds]
    radial = lines[2 * kinds : 2 * kinds + 1] + lines[2 * kinds + 1 : 2 * kinds + 2]
    rows128[...] = jnp.zeros(rows128.shape, F32)
    rows128[0:kinds, :] = bias
    rows128[kinds : kinds + 1, :] = radial
    return jnp.transpose(rows128[...])


def centre_split(centre_t, states, kind, columns, kinds):
    proj = dot(centre_t, states, NT)
    for s in range(kinds):
        proj = proj + jnp.where(kind == float(s), columns[:, s : s + 1], 0.0)
    upper = proj.astype(BF16)
    return upper, (proj - upper.astype(F32)).astype(BF16)


def mine_kernel(
    trips,
    kinds,
    pack,
    edge_col,
    pair_edge,
    w_neigh,
    w_centre,
    w_out,
    gain,
    links,
    pre,
    near,
    w_out_kept,
    gain_kept,
    rows128,
):
    w_out_kept[...] = w_out[...]
    gain_kept[...] = gain[...]
    core = core_bit()
    far = 1 - core
    edges = links.shape[1]
    atoms = edge_col.shape[2]
    scalars = fields(pack[core, core, atoms:], edges, trips, atoms, core)[-1]
    columns = scalar_columns(rows128, scalars, kinds)
    neigh_t = jnp.transpose(w_neigh[...])
    centre_t = jnp.transpose(w_centre[...])

    def row_states(row):
        return [
            edge_col[row, 0],
            pack[core, row, 0:atoms],
            pack[far, row, 0:atoms],
            pair_edge[far, row, 0],
        ]

    mine = row_states(core)
    rows = [
        dot(neigh_t, jnp.concatenate(states, axis=0), NT).astype(BF16)
        for states in (mine, row_states(far))
    ]
    near[...] = rows[0]
    for tile in range(2):
        holder = core if tile == 0 else far
        recv, partner, weight, centre, cell, slot, reach, kind, _ = fields(
            pack[holder, core, atoms:], edges, trips, atoms, core
        )
        links[tile] = link_matrix(recv, partner, weight, edges, atoms)
        upper, lower = centre_split(centre_t, mine[1 + tile], kind, columns, kinds)
        span = slice(tile * atoms, (tile + 3) * atoms)
        values = jnp.concatenate([rows[0][:, span], rows[1][:, span], upper, lower], axis=1)
        pick_centre = onehot(centre, 0, atoms)
        picks = jnp.concatenate(
            [blocked_onehot(slot, cell, range(3, 9), atoms), pick_centre, pick_centre], axis=0
        )
        pre[tile] = dot(values, picks) + columns[:, kinds : kinds + 1] * reach


def inner_slots(tile):
    return [slot for slot in (1, 2) if 0 <= slot - tile < 3]


def remote_kernel(
    trips,
    kinds,
    pack,
    remote,
    pre_mine,
    near_mine,
    w_neigh,
    w_centre,
    links,
    pre_mine_out,
    pre,
    rows128,
):
    core = core_bit()
    far = 1 - core
    edges = links.shape[1]
    atoms = remote.shape[2] - LINES
    scalars = fields(remote[core, far, atoms:], edges, trips, atoms, core)[-1]
    columns = scalar_columns(rows128, scalars, kinds)
    neigh_t = jnp.transpose(w_neigh[...])
    centre_t = jnp.transpose(w_centre[...])
    near_last, near_next = [
        dot(
            neigh_t,
            jnp.concatenate([remote[core, row, 0:atoms], remote[far, row, 0:atoms]], axis=0),
            NT,
        ).astype(BF16)
        for row in (core, far)
    ]
    near_own = near_mine[...]
    for tile in range(2):
        holder = core if tile == 0 else far
        recv, partner, weight, centre, cell, slot, reach, kind, _ = fields(
            remote[holder, far, atoms:], edges, trips, atoms, core
        )
        links[tile] = link_matrix(recv, partner, weight, edges, atoms)
        states = remote[holder, far, 0:atoms]
        inner = [at - tile for at in inner_slots(tile)]
        span = slice(tile * atoms, (tile + 3) * atoms)
        values = jnp.concatenate(
            [
                near_last,
                near_next,
                near_own[:, span],
                *centre_split(centre_t, states, kind, columns, kinds),
            ],
            axis=1,
        )
        pick_centre = onehot(centre, 0, atoms)
        blocks = inner + [3 + at for at in inner] + [6, 7, 8]
        picks = jnp.concatenate(
            [blocked_onehot(slot, cell, blocks, atoms), pick_centre, pick_centre], axis=0
        )
        pre[tile] = dot(values, picks) + columns[:, kinds : kinds + 1] * reach
        _, _, _, _, cell, slot, _, _, _ = fields(
            pack[holder, core, atoms:], edges, trips, atoms, core
        )
        picks = blocked_onehot(slot, cell, inner, atoms)
        pre_mine_out[tile] = pre_mine[tile] + dot(near_next, picks)


def edge_kernel(
    trips,
    pack,
    remote,
    remote_edge,
    links_mine,
    pre_mine,
    links_remote,
    pre_remote,
    w_neigh,
    w_mix,
    post,
    side,
    owned,
):
    core = core_bit()
    far = 1 - core
    edges = links_mine.shape[1]
    atoms = owned.shape[1]
    mix_t = jnp.transpose(w_mix[...])
    corners = [remote_edge[core, core, 0], remote_edge[core, far, 0]]
    corners += [remote_edge[far, core, 0], remote_edge[far, far, 0]]
    near = dot(jnp.transpose(w_neigh[...]), jnp.concatenate(corners, axis=0), NT).astype(BF16)
    jobs = []
    for source, row, links, pre, outer, kept in (
        (pack, core, links_mine, pre_mine, (0,), range(3, 9)),
        (remote, far, links_remote, pre_remote, (0, 3), range(6, 9)),
    ):
        for tile in range(2):
            jobs.append((source, row, links, pre, outer, kept, tile))
    state = [{} for _ in jobs]

    def gather_step(job, held):
        source, row, _, pre, outer, kept, tile = job
        holder = core if tile == 0 else far
        _, _, _, _, cells, slots, reach, _, _ = fields(
            source[holder, row, atoms:], edges, trips, atoms, core
        )
        blocks = [first + 2 * tile for first in outer] + list(kept)
        pick = blocked_onehot(slots, cells, blocks, atoms)
        values = near[:, (2 * tile + 2 - len(outer)) * atoms : (2 * tile + 2) * atoms]
        depth = len(outer) * atoms
        held["total"] = pre[tile] + dot(values, pick[0:depth])
        held["pick"] = pick[depth:]
        held["envelope"] = (1.0 - reach * reach) ** 2

    def feature_step(job, held):
        total = held["total"]
        feat = (0.5 * total * (1.0 + jnp.tanh(0.5 * total)) * held["envelope"]).astype(BF16)
        held["feat"] = feat
        held["mixed"] = dot(mix_t, feat).astype(BF16)

    def message_step(job, held):
        message = held["feat"].astype(F32) * dot(held["mixed"], job[2][job[6]])
        held["message"] = message.astype(BF16)

    def spread_step(job, held):
        held["spread"] = dot(held["pick"], held["message"], NT)

    steps = (gather_step, feature_step, message_step, spread_step)
    for turn in range(len(jobs) + len(steps) - 1):
        for i, step in reversed(list(enumerate(steps))):
            if 0 <= turn - i < len(jobs):
                step(jobs[turn - i], state[turn - i])
    spreads = [held["spread"] for held in state]

    def cell(row, slot):
        total = None
        for tile in range(2):
            if 0 <= slot - tile < 3:
                parts = [spreads[tile][(3 * row + slot - tile) * atoms :][:atoms]]
                if row == 0:
                    parts.append(spreads[2 + tile][(slot - tile) * atoms :][:atoms])
                for part in parts:
                    total = part if total is None else total + part
        return total

    for row, at in ((0, core), (1, far)):
        side[at] = cell(row, 0).astype(BF16)
        owned[at] = cell(row, 1)
        post[0, at] = cell(row, 2).astype(BF16)
        post[1, at] = cell(row, 3).astype(BF16)


def side_kernel(side, posts, out):
    far = 1 - core_bit()
    out[...] = (side[...].astype(F32) + posts[far, 1].astype(F32)).astype(BF16)


def final_kernel(pack, owned, posts, side, gain, w_out, out):
    core = core_bit()
    far = 1 - core
    atoms = owned.shape[1]
    for row in range(2):
        total = owned[row] + posts[far, 0, row].astype(F32) + side[far, row].astype(F32)
        scale = lax.rsqrt(jnp.mean(total * total, axis=-1, keepdims=True) + 1e-05)
        normed = (total * scale * gain[...]).astype(BF16)
        out[row, 0] = (
            pack[core, row, 0:atoms].astype(F32) + dot(normed, w_out[...])
        ).astype(BF16)


VMEM = pl.BlockSpec(memory_space=pltpu.VMEM)


HBM = pl.BlockSpec(memory_space=pltpu.HBM)


def call(kernel, outs, *operands, scratch=(), specs=None, limit=VMEM_LIMIT):
    return pl.pallas_call(
        kernel,
        out_shape=outs,
        in_specs=specs or [VMEM] * len(operands),
        out_specs=jax.tree.map(lambda _: VMEM, outs),
        scratch_shapes=list(scratch),
        compiler_params=pltpu.CompilerParams(vmem_limit_bytes=limit),
    )(*operands)


def pairings():
    count_x, count_y = lax.axis_size("gx"), lax.axis_size("gy")
    along_y, along_x = [], []
    for y in range(0, count_y, 2):
        first, second = (y + 2) % count_y, y + 1
        along_y += [(first, second), (second, first)]
    for x in range(count_x):
        for y in range(0, count_y, 2):
            first, second = (x + 1) % count_x * count_y + y, x * count_y + y + 1
            along_x += [(first, second), (second, first)]
    chips = [[y, y + 1] for y in range(0, count_y, 2)]
    return along_y, along_x, chips


def body(
    state,
    species,
    species_bias,
    edge_index,
    edge_count,
    edge_dist,
    trip_index,
    trip_count,
    trip_cos,
    radial_weight,
    norm_gain,
    w_centre,
    w_neigh,
    w_mix,
    w_out,
):
    size_x, _, atoms, chans = state.shape
    edges = edge_index.shape[3]
    trips = trip_index.shape[3]
    kinds = species_bias.shape[0]
    along_y, along_x, chips = pairings()
    both = ("gx", "gy")

    def gathered(value):
        return lax.all_gather(value, "gy", axis_index_groups=chips)

    def shaped(*shape, dtype=BF16):
        return jax.ShapeDtypeStruct(shape, dtype)

    edge_col = lax.ppermute(state, "gy", along_y)
    radial = radial_weight.reshape(1, chans)
    packed = call(
        pack_kernel,
        shaped(size_x, atoms + LINES, chans),
        edge_count.reshape(size_x),
        trip_count.reshape(size_x),
        state,
        edge_index,
        edge_dist,
        trip_index,
        trip_cos,
        species,
        species_bias,
        radial,
        specs=[HBM] * 10,
        limit=VMEM_ALL,
        scratch=[
            pltpu.VMEM((LINES, chans), F32),
            pltpu.SMEM((size_x,), jnp.int32),
            pltpu.SMEM((size_x,), jnp.int32),
            *(
                pltpu.VMEM(each.shape, each.dtype)
                for each in (
                    edge_index,
                    edge_dist,
                    trip_index,
                    trip_cos,
                    species,
                    species_bias,
                    radial,
                )
            ),
            pltpu.SemaphoreType.DMA((11,)),
        ],
    )
    pack = gathered(packed)
    remote = lax.ppermute(pack, both, along_x)
    pair_edge = gathered(edge_col)
    remote_edge = lax.ppermute(pair_edge, both, along_x)
    links = shaped(2, edges, edges)
    pre = shaped(2, chans, edges, dtype=F32)
    links_mine, pre_mine, near_mine, w_out, gain = call(
        functools.partial(mine_kernel, trips, kinds),
        (
            links,
            pre,
            shaped(chans, 4 * atoms),
            shaped(*w_out.shape),
            shaped(1, chans, dtype=F32),
        ),
        pack,
        edge_col,
        pair_edge,
        w_neigh,
        w_centre,
        w_out,
        norm_gain.reshape(1, chans),
        scratch=[pltpu.VMEM((128, chans), F32)],
    )
    links_remote, pre_mine, pre_remote = call(
        functools.partial(remote_kernel, trips, kinds),
        (links, pre, pre),
        pack,
        remote,
        pre_mine,
        near_mine,
        w_neigh,
        w_centre,
        scratch=[pltpu.VMEM((128, chans), F32)],
    )
    tile = (atoms, chans)
    post, side, owned = call(
        functools.partial(edge_kernel, trips),
        (shaped(2, 2, *tile), shaped(2, *tile), shaped(2, *tile, dtype=F32)),
        pack,
        remote,
        remote_edge,
        links_mine,
        pre_mine,
        links_remote,
        pre_remote,
        w_neigh,
        w_mix,
    )
    posts = gathered(post)
    side_out = call(side_kernel, shaped(2, *tile), side, posts)
    side_in = lax.all_gather(side_out, "gy", axis_index_groups=[list(pair) for pair in along_y[::2]])
    return call(
        final_kernel,
        shaped(*state.shape),
        pack,
        owned,
        posts,
        side_in,
        gain,
        w_out,
    )


def solution(mesh):
    placed = (
        P("gx", "gy", None, None),
        P("gx", "gy", None),
        P(),
        P("gx", "gy", None, None),
        P("gx", "gy"),
        P("gx", "gy", None),
        P("gx", "gy", None, None),
        P("gx", "gy"),
        P("gx", "gy", None),
        P(),
        P(),
        P(),
        P(),
        P(),
        P(),
    )
    return jax.shard_map(
        body, mesh=mesh, in_specs=placed, out_specs=P("gx", "gy", None, None), check_vma=False
    )
```

```python
import functools

import jax
import jax.numpy as jnp
from jax import lax
from jax.experimental import pallas as pl
from jax.experimental.pallas import tpu as pltpu
from jax.sharding import PartitionSpec as P


F32 = jnp.float32
BF16 = jnp.bfloat16
NT = (((1,), (1,)), ((), ()))
TN = (((0,), (0,)), ((), ()))
VMEM_LIMIT = 32 * 1024 * 1024
VMEM_ALL = 63 * 1024 * 1024
LINES = 48


def core_bit():
    return lax.rem(lax.axis_index("gy"), 2)


def dot(left, right, dims=(((1,), (0,)), ((), ()))):
    return lax.dot_general(left, right, dims, preferred_element_type=F32)


def onehot(index, first, count):
    rows = lax.broadcasted_iota(jnp.int32, (count, index.shape[1]), 0) + first
    return jnp.where(rows == index, 1.0, 0.0).astype(BF16)


def blocked_onehot(low, high, blocks, size, values=1.0):
    base = onehot(low, 0, size)
    return jnp.concatenate(
        [base * jnp.where(high == b, values, 0.0).astype(BF16) for b in blocks],
        axis=0,
    )


def fields(block, edges, trips, atoms, core):
    lines = block.astype(F32)
    width = lines.shape[1]
    at = 0

    def take(length):
        nonlocal at
        count = length // width
        parts = [lines[at + i : at + i + 1] for i in range(count)]
        at += count
        return jnp.concatenate(parts, axis=1)

    half = float(edges // 2)
    recv = (take(trips) + half).astype(jnp.int32)
    partner = (take(trips) + half).astype(jnp.int32)
    weight = take(trips)
    centre = take(edges).astype(jnp.int32)
    cell = take(edges)
    cell = jnp.where(core == 1, 8.0 - cell, cell)
    cell = cell.astype(jnp.int32)
    slot = take(edges).astype(jnp.int32)
    reach = take(edges)
    reach = reach + take(edges)
    kind = lines[at : at + 1, 0:atoms]
    return recv, partner, weight, centre, cell, slot, reach, kind, lines[at + 1 :]


def pack_kernel(
    count_e_hbm,
    count_t_hbm,
    state_hbm,
    index_e_hbm,
    dist_hbm,
    index_t_hbm,
    cosine_hbm,
    species_hbm,
    bias_hbm,
    radial_hbm,
    out,
    lines,
    count_e,
    count_t,
    index_e,
    dist,
    index_t,
    cosine,
    species,
    bias,
    radial,
    sems,
):
    edges = dist.shape[2]
    trips = cosine.shape[2]
    atoms = species.shape[2]
    width = lines.shape[1]
    half = edges // 2
    copies = [
        (count_e_hbm, count_e),
        (count_t_hbm, count_t),
        (index_e_hbm, index_e),
        (dist_hbm, dist),
        (index_t_hbm, index_t),
        (cosine_hbm, cosine),
        (species_hbm, species),
        (bias_hbm, bias),
        (radial_hbm, radial),
    ]
    copies += [(state_hbm.at[row, 0], out.at[row, pl.ds(0, atoms)]) for row in range(2)]
    copies = [
        pltpu.make_async_copy(source, target, sems.at[i])
        for i, (source, target) in enumerate(copies)
    ]
    for copy in copies:
        copy.start()
    lanes_e = lax.broadcasted_iota(jnp.int32, (1, edges), 1)
    lanes_t = lax.broadcasted_iota(jnp.int32, (1, trips), 1)
    lines[...] = jnp.zeros(lines.shape, F32)
    for copy in copies[:-2]:
        copy.wait()
    for row in range(2):
        at = 0

        def put(values):
            nonlocal at
            for first in range(0, values.shape[1], width):
                lines[at : at + 1, :] = values[:, first : first + width]
                at += 1

        put((index_t[row, 0, 0:1, :] - half).astype(F32))
        put((index_t[row, 0, 1:2, :] - half).astype(F32))
        put(jnp.where(lanes_t < count_t[row], cosine[row], 0.0))
        put(index_e[row, 0, 0:1, :].astype(F32))
        code = index_e[row, 0, 1:2, :].astype(F32)
        cell = jnp.floor(code * (1.0 / atoms))
        put(cell)
        put(code - cell * float(atoms))
        reach = jnp.where(lanes_e < count_e[row], dist[row], 1.0)
        upper = reach.astype(BF16).astype(F32)
        put(upper)
        put(reach - upper)
        lines[at : at + 1, 0:atoms] = species[row].astype(F32)
        at += 1
        for values in (bias[...], radial[...]):
            upper = values.astype(BF16).astype(F32)
            for each in (upper, values - upper):
                lines[at : at + values.shape[0], :] = each
                at += values.shape[0]
        out[row, atoms : atoms + LINES] = lines[...].astype(BF16)
    for copy in copies[-2:]:
        copy.wait()


def link_factors(recv, partner, weight, edges, atoms):
    blocks = range(edges // atoms)

    def parts(index):
        high = lax.div(index, atoms)
        return index - high * atoms, high

    into = blocked_onehot(*parts(recv), blocks, atoms)
    out_of = blocked_onehot(*parts(partner), blocks, atoms, weight)
    return out_of, into


def scalar_columns(rows128, lines, kinds):
    bias = lines[0:kinds] + lines[kinds : 2 * kinds]
    radial = lines[2 * kinds : 2 * kinds + 1] + lines[2 * kinds + 1 : 2 * kinds + 2]
    rows128[...] = jnp.zeros(rows128.shape, F32)
    rows128[0:kinds, :] = bias
    rows128[kinds : kinds + 1, :] = radial
    return jnp.transpose(rows128[...])


def centre_split(centre_t, states, kind, columns, kinds):
    proj = dot(centre_t, states, NT)
    for s in range(kinds):
        proj = proj + jnp.where(kind == float(s), columns[:, s : s + 1], 0.0)
    upper = proj.astype(BF16)
    return upper, (proj - upper.astype(F32)).astype(BF16)


def mine_kernel(
    trips,
    kinds,
    pack,
    edge_col,
    pair_edge,
    w_neigh,
    w_centre,
    w_out,
    gain,
    links,
    pre,
    near,
    w_out_kept,
    gain_kept,
    rows128,
):
    w_out_kept[...] = w_out[...]
    gain_kept[...] = gain[...]
    core = core_bit()
    far = 1 - core
    edges = links.shape[1]
    atoms = edge_col.shape[2]
    scalars = fields(pack[core, core, atoms:], edges, trips, atoms, core)[-1]
    columns = scalar_columns(rows128, scalars, kinds)
    neigh_t = jnp.transpose(w_neigh[...])
    centre_t = jnp.transpose(w_centre[...])

    def row_states(row):
        return [
            edge_col[row, 0],
            pack[core, row, 0:atoms],
            pack[far, row, 0:atoms],
            pair_edge[far, row, 0],
        ]

    mine = row_states(core)
    rows = [
        dot(neigh_t, jnp.concatenate(states, axis=0), NT).astype(BF16)
        for states in (mine, row_states(far))
    ]
    near[...] = rows[0]
    held = None

    def finish(tile, values, picks, reach):
        pre[tile] = dot(values, picks) + columns[:, kinds : kinds + 1] * reach

    for tile in range(2):
        holder = core if tile == 0 else far
        recv, partner, weight, centre, cell, slot, reach, kind, _ = fields(
            pack[holder, core, atoms:], edges, trips, atoms, core
        )
        factors = link_factors(recv, partner, weight, edges, atoms)
        if held is not None:
            finish(*held)
        upper, lower = centre_split(centre_t, mine[1 + tile], kind, columns, kinds)
        span = slice(tile * atoms, (tile + 3) * atoms)
        values = jnp.concatenate([rows[0][:, span], rows[1][:, span], upper, lower], axis=1)
        pick_centre = onehot(centre, 0, atoms)
        picks = jnp.concatenate(
            [blocked_onehot(slot, cell, range(3, 9), atoms), pick_centre, pick_centre], axis=0
        )
        links[tile] = dot(*factors, NT).astype(BF16)
        held = (tile, values, picks, reach)
    finish(*held)


def inner_slots(tile):
    return [slot for slot in (1, 2) if 0 <= slot - tile < 3]


def remote_kernel(
    trips,
    kinds,
    pack,
    remote,
    pre_mine,
    near_mine,
    w_neigh,
    w_centre,
    links,
    pre_mine_out,
    pre,
    rows128,
):
    core = core_bit()
    far = 1 - core
    edges = links.shape[1]
    atoms = remote.shape[2] - LINES
    scalars = fields(remote[core, far, atoms:], edges, trips, atoms, core)[-1]
    columns = scalar_columns(rows128, scalars, kinds)
    neigh_t = jnp.transpose(w_neigh[...])
    centre_t = jnp.transpose(w_centre[...])
    near_last, near_next = [
        dot(
            neigh_t,
            jnp.concatenate([remote[core, row, 0:atoms], remote[far, row, 0:atoms]], axis=0),
            NT,
        ).astype(BF16)
        for row in (core, far)
    ]
    near_own = near_mine[...]
    held = None

    def finish(tile, values, picks, reach):
        pre[tile] = dot(values, picks) + columns[:, kinds : kinds + 1] * reach

    for tile in range(2):
        holder = core if tile == 0 else far
        recv, partner, weight, centre, cell, slot, reach, kind, _ = fields(
            remote[holder, far, atoms:], edges, trips, atoms, core
        )
        factors = link_factors(recv, partner, weight, edges, atoms)
        if held is not None:
            finish(*held)
        states = remote[holder, far, 0:atoms]
        inner = [at - tile for at in inner_slots(tile)]
        span = slice(tile * atoms, (tile + 3) * atoms)
        values = jnp.concatenate(
            [
                near_last,
                near_next,
                near_own[:, span],
                *centre_split(centre_t, states, kind, columns, kinds),
            ],
            axis=1,
        )
        pick_centre = onehot(centre, 0, atoms)
        blocks = inner + [3 + at for at in inner] + [6, 7, 8]
        picks = jnp.concatenate(
            [blocked_onehot(slot, cell, blocks, atoms), pick_centre, pick_centre], axis=0
        )
        links[tile] = dot(*factors, NT).astype(BF16)
        held = (tile, values, picks, reach)
        _, _, _, _, cell, slot, _, _, _ = fields(
            pack[holder, core, atoms:], edges, trips, atoms, core
        )
        picks = blocked_onehot(slot, cell, inner, atoms)
        pre_mine_out[tile] = pre_mine[tile] + dot(near_next, picks)
    finish(*held)


def edge_kernel(
    trips,
    pack,
    remote,
    remote_edge,
    links_mine,
    pre_mine,
    links_remote,
    pre_remote,
    w_neigh,
    w_mix,
    post,
    side,
    owned,
):
    core = core_bit()
    far = 1 - core
    edges = links_mine.shape[1]
    atoms = owned.shape[1]
    mix_t = jnp.transpose(w_mix[...])
    corners = [remote_edge[core, core, 0], remote_edge[core, far, 0]]
    corners += [remote_edge[far, core, 0], remote_edge[far, far, 0]]
    near = dot(jnp.transpose(w_neigh[...]), jnp.concatenate(corners, axis=0), NT).astype(BF16)
    jobs = []
    for source, row, links, pre, outer, kept in (
        (pack, core, links_mine, pre_mine, (0,), range(3, 9)),
        (remote, far, links_remote, pre_remote, (0, 3), range(6, 9)),
    ):
        for tile in range(2):
            jobs.append((source, row, links, pre, outer, kept, tile))
    state = [{} for _ in jobs]

    def gather_step(job, held):
        source, row, _, pre, outer, kept, tile = job
        holder = core if tile == 0 else far
        _, _, _, _, cells, slots, reach, _, _ = fields(
            source[holder, row, atoms:], edges, trips, atoms, core
        )
        blocks = [first + 2 * tile for first in outer] + list(kept)
        pick = blocked_onehot(slots, cells, blocks, atoms)
        values = near[:, (2 * tile + 2 - len(outer)) * atoms : (2 * tile + 2) * atoms]
        depth = len(outer) * atoms
        held["total"] = pre[tile] + dot(values, pick[0:depth])
        held["pick"] = pick[depth:]
        held["envelope"] = (1.0 - reach * reach) ** 2

    def feature_step(job, held):
        total = held["total"]
        feat = (0.5 * total * (1.0 + jnp.tanh(0.5 * total)) * held["envelope"]).astype(BF16)
        held["feat"] = feat
        held["mixed"] = dot(mix_t, feat).astype(BF16)

    def message_step(job, held):
        message = held["feat"].astype(F32) * dot(held["mixed"], job[2][job[6]])
        held["message"] = message.astype(BF16)

    def spread_step(job, held):
        held["spread"] = dot(held["pick"], held["message"], NT)

    steps = (gather_step, feature_step, message_step, spread_step)
    for turn in range(len(jobs) + len(steps) - 1):
        for i, step in reversed(list(enumerate(steps))):
            if 0 <= turn - i < len(jobs):
                step(jobs[turn - i], state[turn - i])
    spreads = [held["spread"] for held in state]

    def cell(row, slot):
        total = None
        for tile in range(2):
            if 0 <= slot - tile < 3:
                parts = [spreads[tile][(3 * row + slot - tile) * atoms :][:atoms]]
                if row == 0:
                    parts.append(spreads[2 + tile][(slot - tile) * atoms :][:atoms])
                for part in parts:
                    total = part if total is None else total + part
        return total

    for row, at in ((0, core), (1, far)):
        side[at] = cell(row, 0).astype(BF16)
        owned[at] = cell(row, 1)
        post[0, at] = cell(row, 2).astype(BF16)
        post[1, at] = cell(row, 3).astype(BF16)


def side_kernel(side, posts, out):
    far = 1 - core_bit()
    out[...] = (side[...].astype(F32) + posts[far, 1].astype(F32)).astype(BF16)


def final_kernel(pack, owned, posts, side, gain, w_out, out):
    core = core_bit()
    far = 1 - core
    atoms = owned.shape[1]
    for row in range(2):
        total = owned[row] + posts[far, 0, row].astype(F32) + side[far, row].astype(F32)
        scale = lax.rsqrt(jnp.mean(total * total, axis=-1, keepdims=True) + 1e-05)
        normed = (total * scale * gain[...]).astype(BF16)
        out[row, 0] = (
            pack[core, row, 0:atoms].astype(F32) + dot(normed, w_out[...])
        ).astype(BF16)


VMEM = pl.BlockSpec(memory_space=pltpu.VMEM)


HBM = pl.BlockSpec(memory_space=pltpu.HBM)


def call(kernel, outs, *operands, scratch=(), specs=None, limit=VMEM_LIMIT):
    return pl.pallas_call(
        kernel,
        out_shape=outs,
        in_specs=specs or [VMEM] * len(operands),
        out_specs=jax.tree.map(lambda _: VMEM, outs),
        scratch_shapes=list(scratch),
        compiler_params=pltpu.CompilerParams(vmem_limit_bytes=limit),
    )(*operands)


def pairings():
    count_x, count_y = lax.axis_size("gx"), lax.axis_size("gy")
    along_y, along_x = [], []
    for y in range(0, count_y, 2):
        first, second = (y + 2) % count_y, y + 1
        along_y += [(first, second), (second, first)]
    for x in range(count_x):
        for y in range(0, count_y, 2):
            first, second = (x + 1) % count_x * count_y + y, x * count_y + y + 1
            along_x += [(first, second), (second, first)]
    chips = [[y, y + 1] for y in range(0, count_y, 2)]
    return along_y, along_x, chips


def body(
    state,
    species,
    species_bias,
    edge_index,
    edge_count,
    edge_dist,
    trip_index,
    trip_count,
    trip_cos,
    radial_weight,
    norm_gain,
    w_centre,
    w_neigh,
    w_mix,
    w_out,
):
    size_x, _, atoms, chans = state.shape
    edges = edge_index.shape[3]
    trips = trip_index.shape[3]
    kinds = species_bias.shape[0]
    along_y, along_x, chips = pairings()
    both = ("gx", "gy")

    def gathered(value):
        return lax.all_gather(value, "gy", axis_index_groups=chips)

    def shaped(*shape, dtype=BF16):
        return jax.ShapeDtypeStruct(shape, dtype)

    edge_col = lax.ppermute(state, "gy", along_y)
    radial = radial_weight.reshape(1, chans)
    packed = call(
        pack_kernel,
        shaped(size_x, atoms + LINES, chans),
        edge_count.reshape(size_x),
        trip_count.reshape(size_x),
        state,
        edge_index,
        edge_dist,
        trip_index,
        trip_cos,
        species,
        species_bias,
        radial,
        specs=[HBM] * 10,
        limit=VMEM_ALL,
        scratch=[
            pltpu.VMEM((LINES, chans), F32),
            pltpu.SMEM((size_x,), jnp.int32),
            pltpu.SMEM((size_x,), jnp.int32),
            *(
                pltpu.VMEM(each.shape, each.dtype)
                for each in (
                    edge_index,
                    edge_dist,
                    trip_index,
                    trip_cos,
                    species,
                    species_bias,
                    radial,
                )
            ),
            pltpu.SemaphoreType.DMA((11,)),
        ],
    )
    pack = gathered(packed)
    remote = lax.ppermute(pack, both, along_x)
    pair_edge = gathered(edge_col)
    remote_edge = lax.ppermute(pair_edge, both, along_x)
    links = shaped(2, edges, edges)
    pre = shaped(2, chans, edges, dtype=F32)
    links_mine, pre_mine, near_mine, w_out, gain = call(
        functools.partial(mine_kernel, trips, kinds),
        (
            links,
            pre,
            shaped(chans, 4 * atoms),
            shaped(*w_out.shape),
            shaped(1, chans, dtype=F32),
        ),
        pack,
        edge_col,
        pair_edge,
        w_neigh,
        w_centre,
        w_out,
        norm_gain.reshape(1, chans),
        scratch=[pltpu.VMEM((128, chans), F32)],
    )
    links_remote, pre_mine, pre_remote = call(
        functools.partial(remote_kernel, trips, kinds),
        (links, pre, pre),
        pack,
        remote,
        pre_mine,
        near_mine,
        w_neigh,
        w_centre,
        scratch=[pltpu.VMEM((128, chans), F32)],
    )
    tile = (atoms, chans)
    post, side, owned = call(
        functools.partial(edge_kernel, trips),
        (shaped(2, 2, *tile), shaped(2, *tile), shaped(2, *tile, dtype=F32)),
        pack,
        remote,
        remote_edge,
        links_mine,
        pre_mine,
        links_remote,
        pre_remote,
        w_neigh,
        w_mix,
    )
    posts = gathered(post)
    side_out = call(side_kernel, shaped(2, *tile), side, posts)
    side_in = lax.all_gather(side_out, "gy", axis_index_groups=[list(pair) for pair in along_y[::2]])
    return call(
        final_kernel,
        shaped(*state.shape),
        pack,
        owned,
        posts,
        side_in,
        gain,
        w_out,
    )


def solution(mesh):
    placed = (
        P("gx", "gy", None, None),
        P("gx", "gy", None),
        P(),
        P("gx", "gy", None, None),
        P("gx", "gy"),
        P("gx", "gy", None),
        P("gx", "gy", None, None),
        P("gx", "gy"),
        P("gx", "gy", None),
        P(),
        P(),
        P(),
        P(),
        P(),
        P(),
    )
    return jax.shard_map(
        body, mesh=mesh, in_specs=placed, out_specs=P("gx", "gy", None, None), check_vma=False
    )
```
